1024 devices in a mesh: fsdp: 32 (over x, z_hi, core), ep: 32 (over y, z_lo).
Axes of the slice: x: 4, y: 8, z: 16 (z_hi: 4, z_lo: 4; z = z_hi * 4 + z_lo), core: 2. Of those that a mesh axis runs over, the one named last changes fastest.
Arguments:
- x_resid: bfloat16 [1024, 64, 2048], P(('fsdp', 'ep')), may hold values from -1.5 to 1.5
- q_latent: bfloat16 [1024, 64, 8, 512], P(('fsdp', 'ep')), may hold values from -3 to 3
- q_rope: bfloat16 [1024, 64, 8, 64], P(('fsdp', 'ep')), may hold values from -27 to 27
- cache_latent: bfloat16 [1024, 64, 512], P(('fsdp', 'ep')), may hold values from -6 to 6
- cache_rope: bfloat16 [1024, 64, 64], P(('fsdp', 'ep')), may hold values from -6 to 6
- new_latent: bfloat16 [1024, 64, 512], P(('fsdp', 'ep')), may hold values from -6 to 6
- new_rope: bfloat16 [1024, 64, 64], P(('fsdp', 'ep')), may hold values from -6 to 6
- w_uv: bfloat16 [512, 8, 128], P('fsdp'), may hold values from -0.25 to 0.25
- w_out: bfloat16 [1024, 2048], P('fsdp'), may hold values from -0.1875 to 0.1875
- norm_gain: float32 [2048], replicated, may hold values from 0.5 to 2
- router: bfloat16 [2048, 32], replicated, may hold values from -0.026516504 to 0.026516504
- expert_ids: int32 [1024, 64, 6], P(('fsdp', 'ep')), may hold values from 0 to 31, all different within a row; in each aligned block of 64 rows (0 to 63, 64 to 127, ..., all dimensions but the last counted through in order) at most 12 rows name the same one
- w_gate: bfloat16 [32, 2048, 704], P('ep'), may hold values from -0.125 to 0.125
- w_up: bfloat16 [32, 2048, 704], P('ep'), may hold values from -0.125 to 0.125
- w_down: bfloat16 [32, 704, 2048], P('ep'), may hold values from -0.21875 to 0.21875
Outputs:
- attended: bfloat16 [1024, 64, 2048], P(('fsdp', 'ep'))
- layer_out: bfloat16 [1024, 64, 2048], P(('fsdp', 'ep'))
The draws below stay inside these ranges and needn't reach their ends.
Inputs may be any that keep to these rules, and one draw needn't show every extreme that they name: `expert_ids`: within the 64 tokens of one sequence every expert is named exactly 12 times.
All inputs are finite; a program needn't handle non-finite values.
Results may differ from the reference program's by a relative error of at most 0.008.
Values may be sent and summed in bfloat16 or wider, within the bound.
A program may use at most 64 MiB of HBM per device.

```python
import math
import jax
import jax.numpy as jnp
import numpy as np
from jax import lax

D = 2048
H = 8
LAT = 512
DR = 64
DV = 128
FFE = 704
TOPK = 6
CACHE = 64
NEW = 64
SEQS = 1024
EXPERTS = 32
CAP = 12


def rope_pair(key):
    key_rope = jnp.clip(jax.random.normal(jax.random.fold_in(key, 12), (SEQS, CACHE, DR), jnp.float32), -6.0, 6.0)
    queries = jnp.clip(jax.random.normal(jax.random.fold_in(key, 13), (SEQS, NEW, H, DR), jnp.float32), -6.0, 6.0)
    return (key_rope, queries)


def draw_cache_rope(key, part):
    key_rope, queries = rope_pair(key)
    return key_rope.astype(jnp.bfloat16)


def draw_q_rope(key, part):
    key_rope, queries = rope_pair(key)
    return queries.astype(jnp.bfloat16)


def draw_router(key, part):
    inverse_root = 1.0 / D ** 0.5
    values = jnp.clip(0.3 * jax.random.normal(jax.random.fold_in(key, 22), (D, EXPERTS), jnp.float32), -1.2, 1.2)
    return (values * inverse_root).astype(jnp.bfloat16)


def steps_of(stream_key, extent, shards, smallest, top_value):
    factor_of, own = 1.0, jax.random.fold_in(stream_key, 6)
    for dim, parts in shards:
        steps = jnp.exp(jax.random.uniform(jax.random.fold_in(own, dim), (parts,), jnp.float32, smallest / len(shards), top_value / len(shards)))
        factor_of = factor_of * jnp.repeat(steps, extent[dim] // parts).reshape([-1 if axis == dim else 1 for axis in range(len(extent))])
    return factor_of


def routed_block(rng, own, number, rows, number_of, top, most, slope):
    order = jax.random.permutation(rng, number_of)
    heavy_load, usual = shares(number_of, rows * top, most, slope, True), shares(number_of, rows * top, most, slope, False)
    places = jnp.arange(number_of)

    def named(tallies, turn):
        used = int((tallies > 0).sum())
        fixed = max(1, used // 4)
        passed = fixed + (places - fixed + turn * (used - fixed)) % max(1, number_of - fixed)
        return jnp.zeros((number_of,), jnp.int32).at[order[jnp.where(places < fixed, places, passed)]].set(jnp.asarray(tallies, jnp.int32))

    tallies = jnp.where(number % 4 == 0, named(heavy_load, number // 4), named(usual, number - number // 4 - 1))
    mixed = jax.random.permutation(jax.random.fold_in(own, 3), number_of)
    source_of, taker = mixed[0:number_of // 2 * 2:2], mixed[1:number_of // 2 * 2:2]
    slack = jnp.minimum(tallies[source_of] - 1, most - tallies[taker]) // 2
    slack = jnp.where((source_of == order[0]) | (taker == order[0]) | (tallies[taker] == 0), 0, jnp.maximum(slack, 0))
    passed = jax.random.randint(jax.random.fold_in(own, 4), (number_of // 2,), 0, 1 << 20) % (slack + 1)
    tallies = tallies.at[source_of].add(-passed).at[taker].add(passed)
    items = jnp.searchsorted(jnp.cumsum(tallies), jnp.arange(rows * top), side="right").astype(jnp.int32)
    listing = items.reshape(top, rows).T
    listing = listing[jax.random.permutation(jax.random.fold_in(own, 1), rows)]
    turn = jax.random.randint(jax.random.fold_in(own, 2), (rows, 1), 0, top)
    return jnp.take_along_axis(listing, (jnp.arange(top)[None, :] + turn) % top, axis=1)


def shares(count, total, limit, skew, full):
    weights = [(1 << 20) // math.isqrt(standing ** skew) + 1 for standing in range(1, count + 1)]
    largest = limit if full else min(limit, max(-(-total // count), total * weights[0] // sum(weights)))
    least = 1 if total - largest >= count - 1 else 0
    counts, rest = [largest] + [least] * (count - 1), total - largest - least * (count - 1)
    while rest > 0:
        free = [i for i in range(1, count) if counts[i] < largest] or [i for i in range(1, count) if counts[i] < limit]
        mass, remaining = sum([weights[i] for i in free]), rest
        for i in free:
            addition = min(limit - counts[i], max(1, remaining * weights[i] // mass), rest)
            counts[i] = counts[i] + addition
            rest = rest - addition
    return np.array(counts)


def noise(stream_key, shape, scale, most, cuts=(), kind=jnp.bfloat16):
    gain = steps_of(stream_key, shape, cuts, -0.22, 0.18) if cuts else 1.0
    array = jax.random.normal(stream_key, shape, jnp.float32) * scale * gain
    return jnp.minimum(jnp.maximum(array, -most), most).astype(kind)


def setup_inputs(seed: int = 0) -> dict:
    splits = jax.random.split(jax.random.key(seed), 16)
    x_resid = noise(splits[0], (SEQS, NEW, D), 0.25, 1.5, ((0, 1024),))
    q_latent = noise(splits[1], (SEQS, NEW, H, LAT), 0.5, 3.0, ((0, 1024),))
    q_rope = draw_q_rope(jax.random.fold_in(splits[15], 71), 0)
    cache_latent = noise(splits[3], (SEQS, CACHE, LAT), 1.0, 6.0, ((0, 1024),))
    cache_rope = draw_cache_rope(jax.random.fold_in(splits[15], 71), 0)
    new_latent = noise(splits[5], (SEQS, NEW, LAT), 1.0, 6.0, ((0, 1024),))
    new_rope = noise(splits[6], (SEQS, NEW, DR), 1.0, 6.0, ((0, 1024),))
    w_uv = noise(splits[7], (LAT, H, DV), LAT ** -0.5, 0.25, ((0, 32),))
    w_out = noise(splits[8], (H * DV, D), (H * DV) ** -0.5, 0.1875, ((0, 32),))
    norm_gain = jnp.clip(jnp.exp(jax.random.uniform(splits[9], (D,), jnp.float32, math.log(0.5), math.log(2.0))), 0.5, 2.0)
    router = draw_router(jax.random.fold_in(splits[15], 71), 0)
    expert_ids_keys = jax.random.split(jax.random.fold_in(splits[11], 1), SEQS * NEW // NEW)
    expert_ids_turns = jax.random.permutation(jax.random.fold_in(splits[11], 3), SEQS * NEW // NEW)
    expert_ids = jax.vmap(lambda own, number: routed_block(jax.random.fold_in(splits[11], 2), own, number, NEW, EXPERTS, TOPK, CAP, 0))(expert_ids_keys, expert_ids_turns).reshape((SEQS, NEW, TOPK))
    w_gate = noise(splits[12], (EXPERTS, D, FFE), D ** -0.5, 0.125, ((0, 32),))
    w_up = noise(splits[13], (EXPERTS, D, FFE), D ** -0.5, 0.125, ((0, 32),))
    w_down = noise(splits[14], (EXPERTS, FFE, D), FFE ** -0.5, 0.21875, ((0, 32),))
    return {"x_resid": x_resid, "q_latent": q_latent, "q_rope": q_rope, "cache_latent": cache_latent, "cache_rope": cache_rope, "new_latent": new_latent, "new_rope": new_rope, "w_uv": w_uv, "w_out": w_out, "norm_gain": norm_gain, "router": router, "expert_ids": expert_ids, "w_gate": w_gate, "w_up": w_up, "w_down": w_down}


softmax_scale = 0.07216878364870323
epsilon = 1e-06

def attend_sequence(q_latent, q_rope, cache_latent, cache_rope, new_latent, new_rope):
    new_count, head_count, latent_width = q_latent.shape
    cache_count = cache_latent.shape[0]
    keys_latent = jnp.concatenate([cache_latent, new_latent], 0)
    keys_rope = jnp.concatenate([cache_rope, new_rope], 0)
    query_rows = q_latent.reshape(new_count * head_count, latent_width)
    rope_rows = q_rope.reshape(new_count * head_count, q_rope.shape[2])
    scores = jnp.dot(query_rows, keys_latent.T, preferred_element_type=jnp.float32)
    scores = (scores + jnp.dot(rope_rows, keys_rope.T, preferred_element_type=jnp.float32)) * softmax_scale
    token_of_row = jnp.arange(new_count * head_count, dtype=jnp.int32) // head_count
    key_index = jnp.arange(keys_latent.shape[0], dtype=jnp.int32)
    visible = key_index[None, :] <= token_of_row[:, None] + cache_count
    row_top = lax.optimization_barrier(jnp.max(jnp.where(visible, scores, -jnp.inf), axis=1, keepdims=True))
    exponent = jnp.where(visible, jnp.exp(scores - row_top), 0.0)
    weights_att = (exponent / lax.optimization_barrier(jnp.sum(exponent, axis=1, keepdims=True))).astype(jnp.bfloat16)
    mixed_latent = jnp.dot(weights_att, keys_latent, preferred_element_type=jnp.float32).astype(jnp.bfloat16)
    return mixed_latent.reshape(new_count, head_count, latent_width)

def before_experts(x_resid, q_latent, q_rope, cache_latent, cache_rope, new_latent, new_rope, expert_ids, w_uv, w_out, norm_gain, router):
    mixed_latent = attend_sequence(q_latent, q_rope, cache_latent, cache_rope, new_latent, new_rope)
    heads_out = jnp.einsum('thl,lhv->thv', mixed_latent.astype(jnp.float32), w_uv.astype(jnp.float32)).astype(jnp.bfloat16)
    heads_flat = heads_out.reshape(mixed_latent.shape[0], -1)
    hidden = x_resid.astype(jnp.float32) + jnp.dot(heads_flat, w_out, preferred_element_type=jnp.float32)
    normed = hidden * lax.rsqrt(lax.optimization_barrier(jnp.mean(hidden * hidden, axis=-1, keepdims=True)) + epsilon)
    normed = (normed * norm_gain.astype(jnp.float32)).astype(jnp.bfloat16)
    logits = jnp.dot(normed, router, preferred_element_type=jnp.float32)
    choose = (expert_ids[..., None] == jnp.arange(EXPERTS, dtype=jnp.int32)).astype(jnp.float32)
    picked = lax.optimization_barrier(jnp.sum(choose * logits[:, None, :], axis=-1))
    gate_weights = jax.nn.softmax(picked, axis=-1)
    assigned = choose.reshape(-1, EXPERTS)
    earlier = jnp.cumsum(assigned, axis=0) - assigned
    slot_index = lax.optimization_barrier(jnp.sum(earlier * assigned, axis=-1)).reshape(expert_ids.shape).astype(jnp.int32)
    return (hidden, normed, gate_weights, slot_index)

def reference(x_resid, q_latent, q_rope, cache_latent, cache_rope, new_latent, new_rope, w_uv, w_out, norm_gain, router, expert_ids, w_gate, w_up, w_down):

    def per_sequence(inputs_seq):
        return before_experts(*inputs_seq, w_uv, w_out, norm_gain, router)
    hidden, normed, gate_weights, slot_index = lax.map(per_sequence, (x_resid, q_latent, q_rope, cache_latent, cache_rope, new_latent, new_rope, expert_ids))
    normed_wide = normed.astype(jnp.float32)
    slot_range = jnp.arange(CAP, dtype=jnp.int32)

    def one_expert(running, inputs_exp):
        gate_w, up_w, down_w, expert = inputs_exp
        is_mine = expert_ids == expert
        matched = (is_mine[..., None] & (slot_index[..., None] == slot_range)).astype(jnp.float32)
        placement_map = lax.optimization_barrier(jnp.sum(matched, axis=2))
        buffers = jnp.einsum('stc,std->scd', placement_map, normed_wide).astype(jnp.bfloat16)
        buffer_rows = buffers.reshape(-1, buffers.shape[2])
        gate_proj = jnp.dot(buffer_rows, gate_w, preferred_element_type=jnp.float32)
        up_proj = jnp.dot(buffer_rows, up_w, preferred_element_type=jnp.float32)
        activated = (jax.nn.silu(gate_proj) * up_proj).astype(jnp.bfloat16)
        result = jnp.dot(activated, down_w, preferred_element_type=jnp.float32).astype(jnp.bfloat16).reshape(buffers.shape)
        combine_weight = lax.optimization_barrier(jnp.sum(matched * gate_weights[..., None], axis=2))
        return (running + jnp.einsum('stc,scd->std', combine_weight, result.astype(jnp.float32)), None)
    routed_sum, _ = lax.scan(one_expert, jnp.zeros(hidden.shape, jnp.float32), (w_gate, w_up, w_down, jnp.arange(EXPERTS, dtype=jnp.int32)))
    return (hidden.astype(jnp.bfloat16), (hidden + routed_sum).astype(jnp.bfloat16))
```

```python
import jax
import jax.numpy as jnp
from jax import lax
from jax.experimental import pallas as pl
from jax.experimental.pallas import tpu as pltpu
from jax.sharding import PartitionSpec as P

softmax_scale = 0.07216878364870323
epsilon = 1e-06
MESH = pl.DeviceIdType.MESH
F32 = jnp.float32
BF = jnp.bfloat16
C = 4
W = 512
CAP = 12
RY = 8


def iota(shape, dim):
    return lax.broadcasted_iota(jnp.int32, shape, dim)


def dot(a, b):
    return jnp.dot(a, b, preferred_element_type=F32)


def dot_t(a, b):
    return lax.dot_general(a, b, (((1,), (1,)), ((), ())), preferred_element_type=F32)


def kernel(
    x_ref, q_ref, qr_ref, cl_ref, cr_ref, nl_ref, nr_ref, wuv_ref, wout_ref, gain_ref, router_ref,
    ids_ref, wg_hbm, wu_hbm, wd_hbm,
    att_ref, out_ref,
    G, wg, wu, wd, KL, KR, MX, HF, HB, NB, MB, WT, SEL, SX, XB, AG, AU, ACT, OB, RB, PS, SB, YB,
    wsem, gz, gx2, gx, gy, gc, ay, am, zf, zb, rs,
):
    f = lax.axis_index("fsdp")
    ep = lax.axis_index("ep")
    x, zh, c = f // 8, (f // 2) % 4, f % 2
    y, zl = ep // 4, ep % 4
    z = zh * 4 + zl

    def dev(dx=0, dy=0, dz=0, dc=0):
        nx, ny, nz, nc = (x + dx + 4) % 4, (y + dy + RY) % RY, (z + dz + 16) % 16, (c + dc) % 2
        return (nx * 8 + (nz // 4) * 2 + nc, ny * 4 + nz % 4)

    sent = []

    def copy(src, dst, sems, idx, to):
        return pltpu.make_async_remote_copy(
            src_ref=src, dst_ref=dst, send_sem=sems.at[(0, *idx)], recv_sem=sems.at[(1, *idx)],
            device_id=to, device_id_type=MESH,
        )

    def send(src, dst, sems, idx, to):
        cp = copy(src, dst, sems, idx, to)
        cp.start()
        sent.append(cp)

    def recv(dst, sems, idx):
        copy(dst, dst, sems, idx, dev(dy=1)).wait_recv()

    two = 2 - 4 * c
    partners = [
        dev(dy=1), dev(dy=-1), dev(dz=1), dev(dz=-1), dev(dz=2), dev(dz=-2), dev(dc=1),
        dev(dx=1), dev(dx=-1), dev(dx=2), dev(dz=4), dev(dz=-4), dev(dz=8),
    ]
    barrier = pltpu.get_barrier_semaphore()
    for to in partners:
        pl.semaphore_signal(barrier, inc=1, device_id=to, device_id_type=MESH)
    loads = [
        pltpu.make_async_copy(wg_hbm, wg, wsem.at[0]),
        pltpu.make_async_copy(wu_hbm, wu, wsem.at[1]),
        pltpu.make_async_copy(wd_hbm, wd, wsem.at[2]),
    ]
    for ld in loads:
        ld.start()
    mine = x * 4 + zh
    G[y, mine, c, 0:16] = wuv_ref[:, pl.ds(pl.multiple_of(y * 128, 128), 128)]
    G[y, mine, c, 16:48] = wout_ref[:, pl.ds(pl.multiple_of(y * 128, 128), 128)]
    G[y, mine, c, 48:80] = wout_ref[:, pl.ds(pl.multiple_of(1024 + y * 128, 128), 128)]
    pl.semaphore_wait(barrier, len(partners))

    own = G.at[y, mine, c]
    for d in range(1, 4):
        send(own, own, gz, (d - 1,), dev(dz=4 * d))

    KL[0:64] = cl_ref[...]
    KL[64:128] = nl_ref[...]
    KR[0:64] = cr_ref[...]
    KR[64:128] = nr_ref[...]
    scores = (dot_t(q_ref[...], KL[...]) + dot_t(qr_ref[...], KR[...])) * softmax_scale
    visible = iota((512, 128), 1) <= (iota((512, 128), 0) >> 3) + 64
    top = jnp.max(jnp.where(visible, scores, -jnp.inf), axis=1, keepdims=True)
    expo = jnp.where(visible, jnp.exp(scores - top), 0.0)
    probs = (expo / jnp.sum(expo, axis=1, keepdims=True)).astype(BF)
    r, cc = iota((512, 512), 0), iota((512, 512), 1)
    perm = jnp.where(cc == ((r & 63) << 3) + (r >> 6), 1.0, 0.0).astype(BF)
    probs = dot(perm, probs).astype(BF)
    MX[...] = dot(probs, KL[...]).astype(BF)

    x2 = (x + 2) % 4

    def unit(j, xx, cx):
        return G.at[j, pl.ds(4 * xx, 4), cx]

    def to_core(j, xx, s, slot):
        u = unit(j, xx, c)
        send(u, u, gc, (s, slot), dev(dc=1))

    def to_x(j, s):
        u = unit(j, x, c)
        send(u, u, gx, (0, s), dev(dx=1))
        send(u, u, gx, (1, s), dev(dx=-1))

    def ring(j, xx, kind, way, s):
        u = unit(j, xx, c)
        send(u, u, gy, (kind, way, s), dev(dy=1 if way == 0 else -1))

    def piece(way, s):
        return (y - s + RY) % RY if way == 0 else (y + s) % RY

    def number(way, s):
        return 0 if s == 0 else (s if way == 0 else 4 + s)

    steps = [[4, 3], [3, 4]]
    for d in range(1, 4):
        recv(own, gz, (d - 1,))
    u0 = unit(y, x, c)
    send(u0, u0, gx2, (0,), dev(dx=2))
    for way in range(2):
        ring(y, x, 0, way, 0)
    to_x(y, 0)
    to_core(y, x, 0, 0)
    recv(unit(y, x2, c), gx2, (0,))
    for way in range(2):
        ring(y, x2, 1, way, 0)
    to_core(y, x2, 0, 1)

    def took_x(j, s):
        for i, xx in ((0, (x + 3) % 4), (1, (x + 1) % 4)):
            recv(unit(j, xx, c), gx, (i, s))
            to_core(j, xx, s, 2 + i)

    def slot_of(way, s, kind):
        return s if way == 0 else RY - s

    for s in range(1, 5):
        for kind in range(2):
            xx = x if kind == 0 else x2
            for way in range(2):
                if s > steps[kind][way]:
                    continue
                j = piece(way, s)
                recv(unit(j, xx, c), gy, (kind, way, s - 1))
                if s < steps[kind][way]:
                    ring(j, xx, kind, way, s)
                n = slot_of(way, s, kind)
                if kind == 0:
                    to_x(j, n)
                to_core(j, xx, n, kind)
        if s == 1:
            took_x(y, 0)
        else:
            for way in range(2):
                took_x(piece(way, s - 1), slot_of(way, s - 1, 0))
    took_x(piece(0, 4), 4)
    o = 1 - c
    for n in range(RY):
        j = (y - n + RY) % RY
        for slot, xx in ((0, x), (1, x2), (2, (x + 3) % 4), (3, (x + 1) % 4)):
            recv(unit(j, xx, o), gc, (n, slot))

    for h in range(8):
        w = G[h, :, :, 0:16].reshape(512, 128)
        HF[:, 128 * h : 128 * (h + 1)] = dot(MX[64 * h : 64 * (h + 1)], w).astype(BF)
    heads = HF[...]
    square = jnp.zeros((64, 1), F32)
    for half in range(2):
        for j in range(8):
            w = G[j, :, :, 16 + 32 * half : 48 + 32 * half].reshape(1024, 128)
            cols = slice(1024 * half + 128 * j, 1024 * half + 128 * (j + 1))
            hid = x_ref[:, cols].astype(F32) + dot(heads, w)
            HB[:, cols] = hid
            att_ref[:, cols] = hid.astype(BF)
            square = square + jnp.sum(hid * hid, axis=1, keepdims=True)
    inv = lax.rsqrt(square * (1.0 / 2048) + epsilon)
    for k in range(C):
        cols = slice(W * k, W * (k + 1))
        NB[k, y] = (HB[:, cols] * inv * gain_ref[:, cols]).astype(BF)

    far = [[4, 3], [3, 4], [4, 3], [3, 4]]

    def tok(k, way, s):
        b = NB.at[k, piece(way, s)]
        send(b, b, ay, (k, way, s), dev(dy=1 if way == 0 else -1))

    def met(way, s):
        b = MB.at[piece(way, s)]
        send(b, b, am, (way, s), dev(dy=1 if way == 0 else -1))

    for way in range(2):
        tok(0, way, 0)
    logits = jnp.zeros((64, 32), F32)
    for k in range(C):
        logits = logits + dot(NB[k, y], router_ref[W * k : W * (k + 1)])
    e32 = iota((64, 32), 1)
    choose = jnp.zeros((64, 32), F32)
    for k in range(6):
        choose = choose + jnp.where(ids_ref[:, k : k + 1] == e32, 1.0, 0.0)
    chosen = choose > 0.5
    ltop = jnp.max(jnp.where(chosen, logits, -jnp.inf), axis=1, keepdims=True)
    gexp = jnp.where(chosen, jnp.exp(logits - ltop), 0.0)
    gate = gexp / jnp.sum(gexp, axis=1, keepdims=True)
    lower = jnp.where(iota((64, 64), 1) < iota((64, 64), 0), 1.0, 0.0).astype(BF)
    rank = dot(lower, choose.astype(BF))
    rank = jnp.where(chosen, rank, -1.0)
    e0 = jnp.where(iota((32, 128), 0) == iota((32, 128), 1), 1.0, 0.0).astype(BF)
    e1 = jnp.where(iota((32, 128), 0) + 32 == iota((32, 128), 1), 1.0, 0.0).astype(BF)
    MB[y] = (dot(rank.astype(BF), e0) + dot(gate.astype(BF), e1)).astype(BF)
    for way in range(2):
        met(way, 0)

    offs = [0, 1, -1, two]

    def plan():
        lane = iota((64, 128), 1)
        for i in range(4):
            e = 4 * y + (zl + offs[i] + 4) % 4
            for j in range(RY):
                m = MB[j].astype(F32)
                a = jnp.sum(jnp.where(lane == e, m, 0.0), axis=1, keepdims=True)
                g = jnp.sum(jnp.where(lane == e + 32, m, 0.0), axis=1, keepdims=True)
                hit = (a > -0.5) & (lane.astype(F32) == a + float(CAP * j))
                HOT = jnp.where(hit, 1.0, 0.0)
                WT[i, 64 * j : 64 * (j + 1)] = jnp.where(hit, g, 0.0).astype(BF)
                PS[0, j, :, 128 * i : 128 * (i + 1)] = HOT
        for i in range(4):
            hot = PS[0, :, :, 128 * i : 128 * (i + 1)].reshape(512, 128)
            SEL[i] = hot.T.astype(BF)

    def select(k):
        rows = NB[k].reshape(512, W)
        for i in (1, 2, 3, 0):
            picked = dot(SEL[i, 0:96], rows).astype(BF)
            if i == 0:
                XB[k, 0] = picked
            else:
                SX[k, i - 1] = picked
                send(SX.at[k, i - 1], XB.at[k, i], zf, (k, i - 1), dev(dz=offs[i]))

    def expert(k):
        for i in range(1, 4):
            recv(XB.at[k, i], zf, (k, i - 1))
        if k == 0:
            loads[0].wait()
            loads[1].wait()
        rows = XB[k].reshape(384, W)
        g = dot(rows, wg[W * k : W * (k + 1)])
        u = dot(rows, wu[W * k : W * (k + 1)])
        if k == 0:
            AG[...] = g
            AU[...] = u
        elif k < C - 1:
            AG[...] += g
            AU[...] += u
        else:
            g = AG[...] + g
            u = AU[...] + u
            ACT[...] = (g / (1.0 + jnp.exp(-g)) * u).astype(BF)

    for t in range(C + 5):
        for k in range(C):
            s = t - k
            for way in range(2):
                dist = far[k][way]
                if 1 <= s <= dist:
                    recv(NB.at[k, piece(way, s)], ay, (k, way, s - 1))
                if 0 <= s < dist and (k, s) != (0, 0):
                    tok(k, way, s)
            if k == 0:
                for way in range(2):
                    dist = far[0][way]
                    if 1 <= s <= dist:
                        recv(MB.at[piece(way, s)], am, (way, s - 1))
                    if 1 <= s < dist:
                        met(way, s)
        if t == 4:
            plan()
        if 0 <= t - 4 < C:
            select(t - 4)
        if 0 <= t - 5 < C:
            expert(t - 5)

    loads[2].wait()
    for k in range(C):
        OB[k] = dot(ACT[...], wd[:, W * k : W * (k + 1)]).astype(BF).reshape(4, 96, W)
        for i in range(1, 4):
            send(OB.at[k, i], RB.at[k, i], zb, (k, i - 1), dev(dz=-offs[i]))

    def own_sum(k):
        for i in range(1, 4):
            recv(RB.at[k, i], zb, (k, i - 1))
        total = dot(WT[0, :, 0:96], OB[k, 0])
        for i in range(1, 4):
            total = total + dot(WT[i, :, 0:96], RB[k, i])
        PS[k] = total.reshape(RY, 64, W)

    def take(k, way, s):
        b = YB.at[k, way, s - 1]
        recv(b, rs, (k, way, s - 1))
        return b[...].astype(F32)

    def final(k):
        cols = slice(W * k, W * (k + 1))
        total = HB[:, cols] + PS[k, y]
        for way in range(2):
            total = total + take(k, way, far[k][way])
        out_ref[:, cols] = total.astype(BF)

    for t in range(C + 5):
        if t < C:
            own_sum(t)
        for k in range(C):
            s = t - k
            for way in range(2):
                dist = far[k][way]
                if 0 <= s < dist:
                    dest = (y + dist - s) % RY if way == 0 else (y - dist + s + RY) % RY
                    val = PS[k, dest]
                    if s > 0:
                        val = val + take(k, way, s)
                    SB[k, way, s] = val.astype(BF)
                    send(
                        SB.at[k, way, s], YB.at[k, way, s], rs, (k, way, s),
                        dev(dy=1 if way == 0 else -1),
                    )
            if s == 4:
                final(k)
    for cp in sent:
        cp.wait_send()


def per_device(
    x_resid, q_latent, q_rope, cache_latent, cache_rope, new_latent, new_rope, w_uv, w_out,
    norm_gain, router, expert_ids, w_gate, w_up, w_down,
):
    vmem = pl.BlockSpec(memory_space=pltpu.VMEM)
    anyspace = pl.BlockSpec(memory_space=pl.ANY)
    dma = pltpu.SemaphoreType.DMA
    att, out = pl.pallas_call(
        kernel,
        out_shape=(jax.ShapeDtypeStruct((64, 2048), BF), jax.ShapeDtypeStruct((64, 2048), BF)),
        in_specs=[vmem] * 12 + [anyspace] * 3,
        out_specs=(vmem, vmem),
        scratch_shapes=[
            pltpu.VMEM((8, 16, 2, 80, 128), BF),
            pltpu.VMEM((2048, 704), BF),
            pltpu.VMEM((2048, 704), BF),
            pltpu.VMEM((704, 2048), BF),
            pltpu.VMEM((128, 512), BF),
            pltpu.VMEM((128, 64), BF),
            pltpu.VMEM((512, 512), BF),
            pltpu.VMEM((64, 1024), BF),
            pltpu.VMEM((64, 2048), F32),
            pltpu.VMEM((C, RY, 64, W), BF),
            pltpu.VMEM((RY, 64, 128), BF),
            pltpu.VMEM((4, 512, 128), BF),
            pltpu.VMEM((4, 128, 512), BF),
            pltpu.VMEM((C, 3, 96, W), BF),
            pltpu.VMEM((C, 4, 96, W), BF),
            pltpu.VMEM((384, 704), F32),
            pltpu.VMEM((384, 704), F32),
            pltpu.VMEM((384, 704), BF),
            pltpu.VMEM((C, 4, 96, W), BF),
            pltpu.VMEM((C, 4, 96, W), BF),
            pltpu.VMEM((C, RY, 64, W), F32),
            pltpu.VMEM((C, 2, 4, 64, W), BF),
            pltpu.VMEM((C, 2, 4, 64, W), BF),
            dma((3,)),
            dma((2, 3)),
            dma((2, 1)),
            dma((2, 2, RY)),
            dma((2, 2, 2, 4)),
            dma((2, RY, 4)),
            dma((2, C, 2, 4)),
            dma((2, 2, 4)),
            dma((2, C, 3)),
            dma((2, C, 3)),
            dma((2, C, 2, 4)),
        ],
        compiler_params=pltpu.CompilerParams(
            collective_id=0, has_side_effects=True, vmem_limit_bytes=56 << 20
        ),
    )(
        x_resid[0],
        q_latent.reshape(512, 512),
        q_rope.reshape(512, 64),
        cache_latent[0],
        cache_rope[0],
        new_latent[0],
        new_rope[0],
        w_uv.reshape(16, 1024),
        w_out,
        norm_gain.reshape(1, 2048),
        router,
        expert_ids[0],
        w_gate[0],
        w_up[0],
        w_down[0],
    )
    return att[None], out[None]


def solution(mesh):
    seq = P(("fsdp", "ep"), None, None)
    placed = (
        seq,
        P(("fsdp", "ep"), None, None, None),
        P(("fsdp", "ep"), None, None, None),
        seq,
        seq,
        seq,
        seq,
        P("fsdp", None, None),
        P("fsdp", None),
        P(),
        P(),
        seq,
        P("ep", None, None),
        P("ep", None, None),
        P("ep", None, None),
    )
    return jax.shard_map(
        per_device, mesh=mesh, in_specs=placed, out_specs=(seq, seq), check_vma=False
    )
```

```python
import jax
import jax.numpy as jnp
from jax import lax
from jax.experimental import pallas as pl
from jax.experimental.pallas import tpu as pltpu
from jax.sharding import PartitionSpec as P

softmax_scale = 0.07216878364870323
epsilon = 1e-06
MESH = pl.DeviceIdType.MESH
F32 = jnp.float32
BF = jnp.bfloat16
C = 4
W = 512
PAD = 16
RY = 8


def iota(shape, dim):
    return lax.broadcasted_iota(jnp.int32, shape, dim)


def dot(a, b):
    return jnp.dot(a, b, preferred_element_type=F32)


def dot_t(a, b):
    return lax.dot_general(a, b, (((1,), (1,)), ((), ())), preferred_element_type=F32)


def kernel(
    x_ref, q_ref, qr_ref, cl_ref, cr_ref, nl_ref, nr_ref, wuv_ref, wout_ref, gain_ref, router_ref,
    ids_ref, wg_hbm, wu_hbm, wd_hbm,
    att_ref, out_ref,
    G, wg, wu, wd, KL, KR, PR, MX, HF, HB, NB, MB, WT, X3, SX, XB, OB, RB, PS, SB, YB,
    wsem, gz, gx2, gx, gy, gc, ay, am, zf, zb, rs,
):
    f = lax.axis_index("fsdp")
    ep = lax.axis_index("ep")
    x, zh, c = f // 8, (f // 2) % 4, f % 2
    y, zl = ep // 4, ep % 4
    z = zh * 4 + zl

    def dev(dx=0, dy=0, dz=0, dc=0):
        nx, ny, nz, nc = (x + dx + 4) % 4, (y + dy + RY) % RY, (z + dz + 16) % 16, (c + dc) % 2
        return (nx * 8 + (nz // 4) * 2 + nc, ny * 4 + nz % 4)

    sent = []

    def copy(src, dst, sems, idx, to):
        return pltpu.make_async_remote_copy(
            src_ref=src, dst_ref=dst, send_sem=sems.at[(0, *idx)], recv_sem=sems.at[(1, *idx)],
            device_id=to, device_id_type=MESH,
        )

    def send(src, dst, sems, idx, to):
        cp = copy(src, dst, sems, idx, to)
        cp.start()
        sent.append(cp)

    def recv(dst, sems, idx):
        copy(dst, dst, sems, idx, dev(dy=1)).wait_recv()

    two = 2 - 4 * c
    partners = [
        dev(dy=1), dev(dy=-1), dev(dz=1), dev(dz=-1), dev(dz=2), dev(dz=-2), dev(dc=1),
        dev(dx=1), dev(dx=-1), dev(dx=2), dev(dz=4), dev(dz=-4), dev(dz=8),
    ]
    barrier = pltpu.get_barrier_semaphore()
    for to in partners:
        pl.semaphore_signal(barrier, inc=1, device_id=to, device_id_type=MESH)
    loads = [
        pltpu.make_async_copy(wg_hbm, wg, wsem.at[0]),
        pltpu.make_async_copy(wu_hbm, wu, wsem.at[1]),
        pltpu.make_async_copy(wd_hbm, wd, wsem.at[2]),
    ]
    for ld in loads:
        ld.start()
    mine = x * 4 + zh
    wuv = jnp.where(iota((16, 8, 128), 1) == y, wuv_ref[...].astype(F32), 0.0)
    G[y, mine, c, 0:16] = jnp.sum(wuv, axis=1).astype(BF)
    G[y, mine, c, 16:48] = wout_ref[:, pl.ds(pl.multiple_of(y * 128, 128), 128)]
    G[y, mine, c, 48:80] = wout_ref[:, pl.ds(pl.multiple_of(1024 + y * 128, 128), 128)]
    pl.semaphore_wait(barrier, len(partners))

    own = G.at[y, mine, c]
    for d in range(1, 4):
        send(own, own, gz, (d - 1,), dev(dz=4 * d))

    def attend(n):
        if n == 0:
            KL[0:64] = cl_ref[...]
            KL[64:128] = nl_ref[...]
            KR[0:64] = cr_ref[...]
            KR[64:128] = nr_ref[...]
        rows = slice(128 * n, 128 * (n + 1))
        scores = (dot_t(q_ref[rows], KL[...]) + dot_t(qr_ref[rows], KR[...])) * softmax_scale
        visible = iota((128, 128), 1) <= ((iota((128, 128), 0) + 128 * n) >> 3) + 64
        top = jnp.max(jnp.where(visible, scores, -jnp.inf), axis=1, keepdims=True)
        expo = jnp.where(visible, jnp.exp(scores - top), 0.0)
        PR[rows] = (expo / jnp.sum(expo, axis=1, keepdims=True)).astype(BF)

    def mix(n):
        r, cc = iota((128, 512), 0) + 128 * n, iota((128, 512), 1)
        perm = jnp.where(cc == ((r & 63) << 3) + (r >> 6), 1.0, 0.0).astype(BF)
        part = dot(perm, PR[...]).astype(BF)
        MX[128 * n : 128 * (n + 1)] = dot(part, KL[...]).astype(BF)

    for n in range(2):
        attend(n)

    x2 = (x + 2) % 4

    def unit(j, xx, cx):
        return G.at[j, pl.ds(4 * xx, 4), cx]

    def to_core(j, xx, s, slot):
        u = unit(j, xx, c)
        send(u, u, gc, (s, slot), dev(dc=1))

    def to_x(j, s):
        u = unit(j, x, c)
        send(u, u, gx, (0, s), dev(dx=1))
        send(u, u, gx, (1, s), dev(dx=-1))

    def ring(j, xx, kind, way, s):
        u = unit(j, xx, c)
        send(u, u, gy, (kind, way, s), dev(dy=1 if way == 0 else -1))

    def piece(way, s):
        return (y - s + RY) % RY if way == 0 else (y + s) % RY

    def number(way, s):
        return 0 if s == 0 else (s if way == 0 else 4 + s)

    steps = [[4, 3], [3, 4]]
    for d in range(1, 4):
        recv(own, gz, (d - 1,))
    u0 = unit(y, x, c)
    send(u0, u0, gx2, (0,), dev(dx=2))
    for way in range(2):
        ring(y, x, 0, way, 0)
    for n in range(2, 4):
        attend(n)
    recv(unit(y, x2, c), gx2, (0,))
    for way in range(2):
        ring(y, x2, 1, way, 0)
    to_x(y, 0)
    to_core(y, x, 0, 0)
    to_core(y, x2, 0, 1)

    def took_x(j, s):
        for i, xx in ((0, (x + 3) % 4), (1, (x + 1) % 4)):
            recv(unit(j, xx, c), gx, (i, s))
            to_core(j, xx, s, 2 + i)

    def slot_of(way, s, kind):
        return s if way == 0 else RY - s

    for s in range(1, 5):
        for kind in range(2):
            xx = x if kind == 0 else x2
            for way in range(2):
                if s > steps[kind][way]:
                    continue
                j = piece(way, s)
                recv(unit(j, xx, c), gy, (kind, way, s - 1))
                if s < steps[kind][way]:
                    ring(j, xx, kind, way, s)
                n = slot_of(way, s, kind)
                if kind == 0:
                    to_x(j, n)
                to_core(j, xx, n, kind)
        mix(s - 1)
        if s == 1:
            took_x(y, 0)
        else:
            for way in range(2):
                took_x(piece(way, s - 1), slot_of(way, s - 1, 0))
    took_x(piece(0, 4), 4)
    o = 1 - c
    for n in range(RY):
        j = (y - n + RY) % RY
        for slot, xx in ((0, x), (1, x2), (2, (x + 3) % 4), (3, (x + 1) % 4)):
            recv(unit(j, xx, o), gc, (n, slot))

    for h in range(8):
        w = G[h, :, :, 0:16].reshape(512, 128)
        HF[:, 128 * h : 128 * (h + 1)] = dot(MX[64 * h : 64 * (h + 1)], w).astype(BF)
    heads = HF[...]
    square = jnp.zeros((64, 1), F32)
    for half in range(2):
        for j in range(8):
            w = G[j, :, :, 16 + 32 * half : 48 + 32 * half].reshape(1024, 128)
            cols = slice(1024 * half + 128 * j, 1024 * half + 128 * (j + 1))
            hid = x_ref[:, cols].astype(F32) + dot(heads, w)
            HB[:, cols] = hid
            att_ref[:, cols] = hid.astype(BF)
            square = square + jnp.sum(hid * hid, axis=1, keepdims=True)
    inv = lax.rsqrt(square * (1.0 / 2048) + epsilon)
    for k in range(C):
        cols = slice(W * k, W * (k + 1))
        NB[y, k] = (HB[:, cols] * inv * gain_ref[:, cols]).astype(BF)

    far = [[4, 3], [3, 4], [4, 3], [3, 4]]

    def tok(k, way, s):
        b = NB.at[piece(way, s), k]
        send(b, b, ay, (k, way, s), dev(dy=1 if way == 0 else -1))

    def met(way, s):
        b = MB.at[piece(way, s)]
        send(b, b, am, (way, s), dev(dy=1 if way == 0 else -1))

    for k in range(C):
        for way in range(2):
            tok(k, way, 0)
    logits = jnp.zeros((64, 32), F32)
    for k in range(C):
        logits = logits + dot_t(NB[y, k], router_ref[:, W * k : W * (k + 1)])
    choose_t = jnp.zeros((32, 64), F32)
    for k in range(6):
        choose_t = choose_t + jnp.where(ids_ref[k] == iota((32, 64), 0), 1.0, 0.0)
    eye = jnp.where(iota((64, 64), 1) == iota((64, 64), 0), 1.0, 0.0).astype(BF)
    choose = dot_t(eye, choose_t.astype(BF))
    chosen = choose > 0.5
    ltop = jnp.max(jnp.where(chosen, logits, -jnp.inf), axis=1, keepdims=True)
    gexp = jnp.where(chosen, jnp.exp(logits - ltop), 0.0)
    gate = gexp / jnp.sum(gexp, axis=1, keepdims=True)
    lower = jnp.where(iota((64, 64), 1) < iota((64, 64), 0), 1.0, 0.0).astype(BF)
    rank = dot(lower, choose.astype(BF))
    rank = jnp.where(chosen, rank, -1.0)
    e0 = jnp.where(iota((32, 128), 0) == iota((32, 128), 1), 1.0, 0.0).astype(BF)
    e1 = jnp.where(iota((32, 128), 0) + 32 == iota((32, 128), 1), 1.0, 0.0).astype(BF)
    MB[y] = (dot(rank.astype(BF), e0) + dot(gate.astype(BF), e1)).astype(BF)
    for way in range(2):
        met(way, 0)

    offs = [0, 1, -1, two]
    order = [(0, 0), (0, 1), (1, 1), (0, 2), (1, 2), (0, 3), (1, 3), (0, 4)]

    def select(n):
        j = piece(*order[n])
        lane = iota((64, 128), 1)
        m = MB[j].astype(F32)
        hot = [jnp.zeros((64, 128), F32)] * 4
        weight = [jnp.zeros((64, 128), F32)] * 4
        for i in range(4):
            e = 4 * y + (zl + offs[i] + 4) % 4
            a = jnp.sum(jnp.where(lane == e, m, 0.0), axis=1, keepdims=True)
            g = jnp.sum(jnp.where(lane == e + 32, m, 0.0), axis=1, keepdims=True)
            for v in range(4):
                if v == 0:
                    hit = (a > -0.5) & (lane.astype(F32) == a + float(PAD * i))
                else:
                    d = a - float(4 * (v - 1))
                    hit = (d > -0.5) & (d < 3.5) & (lane.astype(F32) == d + float(PAD * i + 12))
                hot[v] = jnp.where(hit, 1.0, hot[v])
                weight[v] = jnp.where(hit, g, weight[v])
        sel = []
        for v in range(4):
            WT[n, v] = weight[v].astype(BF)
            sel.append(hot[v].T.astype(BF)[0:64])
        last = NB[j, 3]
        for k in range(3):
            cols = slice(W * k, W * (k + 1))
            picked = (dot(sel[0], NB[j, k]) + dot(sel[k + 1], last)).astype(BF)
            XB[n, 0, :, cols] = picked[0:PAD]
            for i in range(1, 4):
                SX[n, i - 1, :, cols] = picked[PAD * i : PAD * (i + 1)]
        for i in range(1, 4):
            send(SX.at[n, i - 1], XB.at[n, i], zf, (n, i - 1), dev(dz=offs[i]))

    def spread(q, back):
        r, cc = iota((64, 64), 1 if back else 0), iota((64, 64), 0 if back else 1)
        hit = ((r >> 4) == (cc >> 4)) & ((cc & 15) >= 12) & ((r & 15) == 4 * q + (cc & 15) - 12)
        return jnp.where(hit, 1.0, 0.0).astype(BF)

    def expert(lo, hi):
        for n in range(lo, hi):
            for i in range(1, 4):
                recv(XB.at[n, i], zf, (n, i - 1))
        if lo == 0:
            for ld in loads:
                ld.wait()
        count = (hi - lo) * 4 * PAD
        for n in range(lo, hi):
            tail = jnp.zeros((64, W), F32)
            for q in range(3):
                tail = tail + dot(spread(q, False), XB[n, :, :, W * q : W * (q + 1)].reshape(64, W))
            X3[n] = tail.astype(BF)
        rows = XB[lo:hi].reshape(count, 1536)
        tail = X3[lo:hi].reshape(count, W)
        g = dot_t(rows, wg[:, 0:1536]) + dot_t(tail, wg[:, 1536:2048])
        u = dot_t(rows, wu[:, 0:1536]) + dot_t(tail, wu[:, 1536:2048])
        act = (g / (1.0 + jnp.exp(-g)) * u).astype(BF)
        X3[lo:hi] = dot(act, wd[:, 1536:2048]).astype(BF).reshape(hi - lo, 64, W)
        front = (iota((64, W), 0) & 15) < 12
        for k in range(3):
            cols = slice(W * k, W * (k + 1))
            part = dot(act, wd[:, cols])
            for n in range(lo, hi):
                own_part = part[64 * (n - lo) : 64 * (n - lo + 1)]
                both = jnp.where(front, own_part, dot(spread(k, True), X3[n]))
                OB[n, :, :, cols] = both.astype(BF).reshape(4, PAD, W)
        for n in reversed(range(lo, hi)):
            for i in range(1, 4):
                send(OB.at[n, i], RB.at[n, i], zb, (n, i - 1), dev(dz=-offs[i]))

    def forward(s):
        for way in range(2):
            if s <= [4, 3][way]:
                recv(MB.at[piece(way, s)], am, (way, s - 1))
                if s < [4, 3][way]:
                    met(way, s)
        for k in range(C):
            for way in range(2):
                dist = far[k][way]
                if s <= dist:
                    recv(NB.at[piece(way, s), k], ay, (k, way, s - 1))
                    if s < dist:
                        tok(k, way, s)

    select(0)
    forward(1)
    select(1)
    select(2)
    forward(2)
    select(3)
    select(4)
    expert(0, 3)
    forward(3)
    select(5)
    select(6)
    expert(3, 5)
    forward(4)
    select(7)
    expert(5, 8)

    def own_sum(n):
        j = piece(*order[n])
        for i in range(1, 4):
            recv(RB.at[n, i], zb, (n, i - 1))
        RB[n, 0] = OB[n, 0]
        tail = jnp.zeros((64, W), F32)
        for k in range(3):
            rows = RB[n, :, :, W * k : W * (k + 1)].reshape(64, W)
            PS[j, k] = dot(WT[n, 0, :, 0:64], rows)
            tail = tail + dot(WT[n, k + 1, :, 0:64], rows)
        PS[j, 3] = tail

    def take(k, way, s):
        b = YB.at[k, way, s - 1]
        recv(b, rs, (k, way, s - 1))
        return b[...].astype(F32)

    def reduce(k, way, s):
        dist = far[k][way]
        if s < dist:
            dest = (y + dist - s) % RY if way == 0 else (y - dist + s + RY) % RY
            val = PS[dest, k]
            if s > 0:
                val = val + take(k, way, s)
            SB[k, way, s] = val.astype(BF)
            send(
                SB.at[k, way, s], YB.at[k, way, s], rs, (k, way, s),
                dev(dy=1 if way == 0 else -1),
            )

    own_sum(7)
    for k in range(C):
        reduce(k, k % 2, 0)
    own_sum(6)
    for k in range(C):
        if k % 2 == 1:
            reduce(k, 0, 0)
    own_sum(5)
    for k in range(C):
        if k % 2 == 0:
            reduce(k, 1, 0)
    for s in range(1, 4):
        for n in ((4, 3), (2, 1), (0,))[s - 1]:
            own_sum(n)
        for k in range(C):
            for way in (k % 2, 1 - k % 2):
                reduce(k, way, s)
    for k in range(C):
        cols = slice(W * k, W * (k + 1))
        total = HB[:, cols] + PS[y, k]
        for way in (1 - k % 2, k % 2):
            total = total + take(k, way, far[k][way])
        out_ref[:, cols] = total.astype(BF)
    for cp in sent:
        cp.wait_send()


def per_device(
    x_resid, q_latent, q_rope, cache_latent, cache_rope, new_latent, new_rope, w_uv, w_out,
    norm_gain, router, expert_ids, w_gate, w_up, w_down,
):
    vmem = pl.BlockSpec(memory_space=pltpu.VMEM)
    anyspace = pl.BlockSpec(memory_space=pl.ANY)
    dma = pltpu.SemaphoreType.DMA
    att, out = pl.pallas_call(
        kernel,
        out_shape=(jax.ShapeDtypeStruct((64, 2048), BF), jax.ShapeDtypeStruct((64, 2048), BF)),
        in_specs=[vmem] * 12 + [anyspace] * 3,
        out_specs=(vmem, vmem),
        scratch_shapes=[
            pltpu.VMEM((8, 16, 2, 80, 128), BF),
            pltpu.VMEM((704, 2048), BF),
            pltpu.VMEM((704, 2048), BF),
            pltpu.VMEM((704, 2048), BF),
            pltpu.VMEM((128, 512), BF),
            pltpu.VMEM((128, 64), BF),
            pltpu.VMEM((512, 128), BF),
            pltpu.VMEM((512, 512), BF),
            pltpu.VMEM((64, 1024), BF),
            pltpu.VMEM((64, 2048), F32),
            pltpu.VMEM((RY, C, 64, W), BF),
            pltpu.VMEM((RY, 64, 128), BF),
            pltpu.VMEM((RY, 4, 64, 128), BF),
            pltpu.VMEM((RY, 64, W), BF),
            pltpu.VMEM((RY, 3, PAD, 1536), BF),
            pltpu.VMEM((RY, 4, PAD, 1536), BF),
            pltpu.VMEM((RY, 4, PAD, 1536), BF),
            pltpu.VMEM((RY, 4, PAD, 1536), BF),
            pltpu.VMEM((RY, C, 64, W), F32),
            pltpu.VMEM((C, 2, 4, 64, W), BF),
            pltpu.VMEM((C, 2, 4, 64, W), BF),
            dma((3,)),
            dma((2, 3)),
            dma((2, 1)),
            dma((2, 2, RY)),
            dma((2, 2, 2, 4)),
            dma((2, RY, 4)),
            dma((2, C, 2, 4)),
            dma((2, 2, 4)),
            dma((2, RY, 3)),
            dma((2, RY, 3)),
            dma((2, C, 2, 4)),
        ],
        compiler_params=pltpu.CompilerParams(
            collective_id=0, has_side_effects=True, vmem_limit_bytes=56 << 20
        ),
    )(
        x_resid[0],
        q_latent.reshape(512, 512),
        q_rope.reshape(512, 64),
        cache_latent[0],
        cache_rope[0],
        new_latent[0],
        new_rope[0],
        w_uv,
        w_out,
        norm_gain.reshape(1, 2048),
        router.T,
        jnp.transpose(expert_ids, (2, 0, 1)),
        w_gate[0].T,
        w_up[0].T,
        w_down[0],
    )
    return att[None], out[None]


def solution(mesh):
    seq = P(("fsdp", "ep"), None, None)
    placed = (
        seq,
        P(("fsdp", "ep"), None, None, None),
        P(("fsdp", "ep"), None, None, None),
        seq,
        seq,
        seq,
        seq,
        P("fsdp", None, None),
        P("fsdp", None),
        P(),
        P(),
        seq,
        P("ep", None, None),
        P("ep", None, None),
        P("ep", None, None),
    )
    return jax.shard_map(
        per_device, mesh=mesh, in_specs=placed, out_specs=(seq, seq), check_vma=False
    )
```

```python
import jax
import jax.numpy as jnp
from jax import lax
from jax.experimental import pallas as pl
from jax.experimental.pallas import tpu as pltpu
from jax.sharding import PartitionSpec as P

softmax_scale = 0.07216878364870323
epsilon = 1e-06
MESH = pl.DeviceIdType.MESH
F32 = jnp.float32
BF = jnp.bfloat16
C = 4
W = 512
PAD = 16
RY = 8


def iota(shape, dim):
    return lax.broadcasted_iota(jnp.int32, shape, dim)


def dot(a, b):
    return jnp.dot(a, b, preferred_element_type=F32)


def dot_t(a, b):
    return lax.dot_general(a, b, (((1,), (1,)), ((), ())), preferred_element_type=F32)


def kernel(
    x_ref, q_ref, qr_ref, cl_ref, cr_ref, nl_ref, nr_ref, wuv_ref, wout_ref, gain_ref, router_ref,
    ids_ref, wg_hbm, wu_hbm, wd_hbm,
    att_ref, out_ref,
    G, wg, wu, wd, KL, KR, PR, MX, HF, HB, NB, MB, WT, X3, SX, XB, OB, RB, PS, SB, YB,
    wsem, gz, gx2, gx, gy, gc, ay, am, zf, zb, rs,
):
    f = lax.axis_index("fsdp")
    ep = lax.axis_index("ep")
    x, zh, c = f // 8, (f // 2) % 4, f % 2
    y, zl = ep // 4, ep % 4
    z = zh * 4 + zl

    def dev(dx=0, dy=0, dz=0, dc=0):
        nx, ny, nz, nc = (x + dx + 4) % 4, (y + dy + RY) % RY, (z + dz + 16) % 16, (c + dc) % 2
        return (nx * 8 + (nz // 4) * 2 + nc, ny * 4 + nz % 4)

    sent = []

    def copy(src, dst, sems, idx, to):
        return pltpu.make_async_remote_copy(
            src_ref=src, dst_ref=dst, send_sem=sems.at[(0, *idx)], recv_sem=sems.at[(1, *idx)],
            device_id=to, device_id_type=MESH,
        )

    def send(src, dst, sems, idx, to):
        cp = copy(src, dst, sems, idx, to)
        cp.start()
        sent.append(cp)

    def recv(dst, sems, idx):
        copy(dst, dst, sems, idx, dev(dy=1)).wait_recv()

    two = 2 - 4 * c
    partners = [
        dev(dy=1), dev(dy=-1), dev(dz=1), dev(dz=-1), dev(dz=2), dev(dz=-2), dev(dc=1),
        dev(dx=1), dev(dx=-1), dev(dx=2), dev(dz=4), dev(dz=-4), dev(dz=8),
    ]
    barrier = pltpu.get_barrier_semaphore()
    for to in partners:
        pl.semaphore_signal(barrier, inc=1, device_id=to, device_id_type=MESH)
    loads = [
        pltpu.make_async_copy(wg_hbm, wg, wsem.at[0]),
        pltpu.make_async_copy(wu_hbm, wu, wsem.at[1]),
        pltpu.make_async_copy(wd_hbm, wd, wsem.at[2]),
    ]
    for ld in loads:
        ld.start()
    mine = x * 4 + zh
    wuv = jnp.where(iota((16, 8, 128), 1) == y, wuv_ref[...].astype(F32), 0.0)
    G[y, mine, c, 0:16] = jnp.sum(wuv, axis=1).astype(BF)
    G[y, mine, c, 16:48] = wout_ref[:, pl.ds(pl.multiple_of(y * 128, 128), 128)]
    G[y, mine, c, 48:80] = wout_ref[:, pl.ds(pl.multiple_of(1024 + y * 128, 128), 128)]
    pl.semaphore_wait(barrier, len(partners))

    own = G.at[y, mine, c]
    x2 = (x + 2) % 4
    facing = G.at[y, x2 * 4 + zh, c]
    send(own, own, gx2, (0,), dev(dx=2))
    for d in range(1, 4):
        send(own, own, gz, (d - 1,), dev(dz=4 * d))

    def attend(n):
        if n == 0:
            KL[0:64] = cl_ref[...]
            KL[64:128] = nl_ref[...]
            KR[0:64] = cr_ref[...]
            KR[64:128] = nr_ref[...]
        rows = slice(128 * n, 128 * (n + 1))
        scores = (dot_t(q_ref[rows], KL[...]) + dot_t(qr_ref[rows], KR[...])) * softmax_scale
        visible = iota((128, 128), 1) <= ((iota((128, 128), 0) + 128 * n) >> 3) + 64
        top = jnp.max(jnp.where(visible, scores, -jnp.inf), axis=1, keepdims=True)
        expo = jnp.where(visible, jnp.exp(scores - top), 0.0)
        PR[rows] = (expo / jnp.sum(expo, axis=1, keepdims=True)).astype(BF)

    def mix(n):
        r, cc = iota((128, 512), 0) + 128 * n, iota((128, 512), 1)
        perm = jnp.where(cc == ((r & 63) << 3) + (r >> 6), 1.0, 0.0).astype(BF)
        part = dot(perm, PR[...]).astype(BF)
        MX[128 * n : 128 * (n + 1)] = dot(part, KL[...]).astype(BF)

    for n in range(2):
        attend(n)

    recv(facing, gx2, (0,))
    for d in range(1, 4):
        send(facing, facing, gz, (2 + d,), dev(dz=4 * d))

    def unit(j, xx, cx):
        return G.at[j, pl.ds(4 * xx, 4), cx]

    def to_core(j, xx, s, slot):
        u = unit(j, xx, c)
        send(u, u, gc, (s, slot), dev(dc=1))

    def to_x(j, s):
        u = unit(j, x, c)
        send(u, u, gx, (0, s), dev(dx=1))
        send(u, u, gx, (1, s), dev(dx=-1))

    def ring(j, xx, kind, way, s):
        u = unit(j, xx, c)
        send(u, u, gy, (kind, way, s), dev(dy=1 if way == 0 else -1))

    def piece(way, s):
        return (y - s + RY) % RY if way == 0 else (y + s) % RY

    def number(way, s):
        return 0 if s == 0 else (s if way == 0 else 4 + s)

    steps = [[4, 3], [3, 4]]
    for d in range(1, 4):
        recv(own, gz, (d - 1,))
    for way in range(2):
        ring(y, x, 0, way, 0)
    attend(2)
    for d in range(1, 4):
        recv(facing, gz, (2 + d,))
    for way in range(2):
        ring(y, x2, 1, way, 0)
    to_x(y, 0)
    to_core(y, x, 0, 0)
    to_core(y, x2, 0, 1)
    attend(3)

    def took_x(j, s):
        for i, xx in ((0, (x + 3) % 4), (1, (x + 1) % 4)):
            recv(unit(j, xx, c), gx, (i, s))
            to_core(j, xx, s, 2 + i)

    def slot_of(way, s, kind):
        return s if way == 0 else RY - s

    for s in range(1, 5):
        for kind in range(2):
            xx = x if kind == 0 else x2
            for way in range(2):
                if s > steps[kind][way]:
                    continue
                j = piece(way, s)
                recv(unit(j, xx, c), gy, (kind, way, s - 1))
                if s < steps[kind][way]:
                    ring(j, xx, kind, way, s)
                n = slot_of(way, s, kind)
                if kind == 0:
                    to_x(j, n)
                to_core(j, xx, n, kind)
        mix(s - 1)
        if s == 1:
            took_x(y, 0)
        else:
            for way in range(2):
                took_x(piece(way, s - 1), slot_of(way, s - 1, 0))
    took_x(piece(0, 4), 4)
    o = 1 - c
    for n in range(RY):
        j = (y - n + RY) % RY
        for slot, xx in ((0, x), (1, x2), (2, (x + 3) % 4), (3, (x + 1) % 4)):
            recv(unit(j, xx, o), gc, (n, slot))

    for h in range(8):
        w = G[h, :, :, 0:16].reshape(512, 128)
        HF[:, 128 * h : 128 * (h + 1)] = dot(MX[64 * h : 64 * (h + 1)], w).astype(BF)
    heads = HF[...]
    square = jnp.zeros((64, 1), F32)
    for half in range(2):
        for j in range(8):
            w = G[j, :, :, 16 + 32 * half : 48 + 32 * half].reshape(1024, 128)
            cols = slice(1024 * half + 128 * j, 1024 * half + 128 * (j + 1))
            hid = x_ref[:, cols].astype(F32) + dot(heads, w)
            HB[:, cols] = hid
            att_ref[:, cols] = hid.astype(BF)
            square = square + jnp.sum(hid * hid, axis=1, keepdims=True)
    inv = lax.rsqrt(square * (1.0 / 2048) + epsilon)
    for k in range(C):
        cols = slice(W * k, W * (k + 1))
        NB[y, k] = (HB[:, cols] * inv * gain_ref[:, cols]).astype(BF)

    far = [[4, 3], [3, 4], [4, 3], [3, 4]]

    def tok(k, way, s):
        b = NB.at[piece(way, s), k]
        send(b, b, ay, (k, way, s), dev(dy=1 if way == 0 else -1))

    def met(way, s):
        b = MB.at[piece(way, s)]
        send(b, b, am, (way, s), dev(dy=1 if way == 0 else -1))

    for k in range(C):
        for way in range(2):
            tok(k, way, 0)
    logits = jnp.zeros((64, 32), F32)
    for k in range(C):
        logits = logits + dot_t(NB[y, k], router_ref[:, W * k : W * (k + 1)])
    choose_t = jnp.zeros((32, 64), F32)
    for k in range(6):
        choose_t = choose_t + jnp.where(ids_ref[k] == iota((32, 64), 0), 1.0, 0.0)
    eye = jnp.where(iota((64, 64), 1) == iota((64, 64), 0), 1.0, 0.0).astype(BF)
    choose = dot_t(eye, choose_t.astype(BF))
    chosen = choose > 0.5
    ltop = jnp.max(jnp.where(chosen, logits, -jnp.inf), axis=1, keepdims=True)
    gexp = jnp.where(chosen, jnp.exp(logits - ltop), 0.0)
    gate = gexp / jnp.sum(gexp, axis=1, keepdims=True)
    lower = jnp.where(iota((64, 64), 1) < iota((64, 64), 0), 1.0, 0.0).astype(BF)
    rank = dot(lower, choose.astype(BF))
    rank = jnp.where(chosen, rank, -1.0)
    e0 = jnp.where(iota((32, 128), 0) == iota((32, 128), 1), 1.0, 0.0).astype(BF)
    e1 = jnp.where(iota((32, 128), 0) + 32 == iota((32, 128), 1), 1.0, 0.0).astype(BF)
    MB[y] = (dot(rank.astype(BF), e0) + dot(gate.astype(BF), e1)).astype(BF)
    for way in range(2):
        met(way, 0)

    offs = [0, 1, -1, two]
    order = [(0, 0), (0, 1), (1, 1), (0, 2), (1, 2), (0, 3), (1, 3), (0, 4)]

    lane = iota((128, 128), 1)
    src = iota((128, 128), 0)
    block = (lane >> 4) & 3
    step = jnp.where(block == 1, 1, jnp.where(block == 2, -1, jnp.where(block == 3, two, 0)))
    wanted = 4 * y + ((zl + step + 4) & 3)
    pick_rank = jnp.where(src == wanted, 1.0, 0.0).astype(BF)
    pick_gate = jnp.where(src == wanted + 32, 1.0, 0.0).astype(BF)
    lane = iota((64, 128), 1)
    low = lane & 15
    places = [jnp.where(low < 12, low, -9)]
    for q in range(3):
        places.append(jnp.where(low >= 12, low - 12 + 4 * q, -9))
    places = [p.astype(F32) for p in places]

    def select(n):
        j = piece(*order[n])
        m = MB[j]
        ranks, gates = dot(m, pick_rank), dot(m, pick_gate)
        sel = []
        for v in range(4):
            hit = ranks == places[v]
            WT[n, v] = jnp.where(hit, gates, 0.0).astype(BF)
            sel.append(jnp.where(hit, 1.0, 0.0).T.astype(BF)[0:64])
        last = NB[j, 3]
        for k in range(3):
            cols = slice(W * k, W * (k + 1))
            picked = (dot(sel[0], NB[j, k]) + dot(sel[k + 1], last)).astype(BF)
            XB[n, 0, :, cols] = picked[0:PAD]
            for i in range(1, 4):
                SX[n, i - 1, :, cols] = picked[PAD * i : PAD * (i + 1)]
        for i in range(1, 4):
            send(SX.at[n, i - 1], XB.at[n, i], zf, (n, i - 1), dev(dz=offs[i]))

    def spread(q, back):
        r, cc = iota((64, 64), 1 if back else 0), iota((64, 64), 0 if back else 1)
        hit = ((r >> 4) == (cc >> 4)) & ((cc & 15) >= 12) & ((r & 15) == 4 * q + (cc & 15) - 12)
        return jnp.where(hit, 1.0, 0.0).astype(BF)

    def expert(lo, hi):
        for n in range(lo, hi):
            for i in range(1, 4):
                recv(XB.at[n, i], zf, (n, i - 1))
        if lo == 0:
            for ld in loads:
                ld.wait()
        count = (hi - lo) * 4 * PAD
        for n in range(lo, hi):
            tail = jnp.zeros((64, W), F32)
            for q in range(3):
                tail = tail + dot(spread(q, False), XB[n, :, :, W * q : W * (q + 1)].reshape(64, W))
            X3[n] = tail.astype(BF)
        rows = XB[lo:hi].reshape(count, 1536)
        tail = X3[lo:hi].reshape(count, W)
        g = dot_t(rows, wg[:, 0:1536]) + dot_t(tail, wg[:, 1536:2048])
        u = dot_t(rows, wu[:, 0:1536]) + dot_t(tail, wu[:, 1536:2048])
        act = (g / (1.0 + jnp.exp(-g)) * u).astype(BF)
        X3[lo:hi] = dot(act, wd[:, 1536:2048]).astype(BF).reshape(hi - lo, 64, W)
        front = (iota((64, W), 0) & 15) < 12
        for k in range(3):
            cols = slice(W * k, W * (k + 1))
            part = dot(act, wd[:, cols])
            for n in range(lo, hi):
                own_part = part[64 * (n - lo) : 64 * (n - lo + 1)]
                both = jnp.where(front, own_part, dot(spread(k, True), X3[n]))
                OB[n, :, :, cols] = both.astype(BF).reshape(4, PAD, W)
        for n in reversed(range(lo, hi)):
            for i in range(1, 4):
                send(OB.at[n, i], RB.at[n, i], zb, (n, i - 1), dev(dz=-offs[i]))

    def forward(s):
        for way in range(2):
            if s <= [4, 3][way]:
                recv(MB.at[piece(way, s)], am, (way, s - 1))
                if s < [4, 3][way]:
                    met(way, s)
        for k in range(C):
            for way in range(2):
                dist = far[k][way]
                if s <= dist:
                    recv(NB.at[piece(way, s), k], ay, (k, way, s - 1))
                    if s < dist:
                        tok(k, way, s)

    select(0)
    forward(1)
    select(1)
    select(2)
    forward(2)
    select(3)
    select(4)
    forward(3)
    select(5)
    select(6)
    expert(0, 3)
    forward(4)
    select(7)
    expert(3, 5)
    expert(5, 8)

    def own_sum(n):
        j = piece(*order[n])
        for i in range(1, 4):
            recv(RB.at[n, i], zb, (n, i - 1))
        RB[n, 0] = OB[n, 0]
        tail = jnp.zeros((64, W), F32)
        for k in range(3):
            rows = RB[n, :, :, W * k : W * (k + 1)].reshape(64, W)
            PS[j, k] = dot(WT[n, 0, :, 0:64], rows)
            tail = tail + dot(WT[n, k + 1, :, 0:64], rows)
        PS[j, 3] = tail

    def take(k, way, s):
        b = YB.at[k, way, s - 1]
        recv(b, rs, (k, way, s - 1))
        return b[...].astype(F32)

    def reduce(k, way, s):
        dist = far[k][way]
        if s < dist:
            dest = (y + dist - s) % RY if way == 0 else (y - dist + s + RY) % RY
            val = PS[dest, k]
            if s > 0:
                val = val + take(k, way, s)
            SB[k, way, s] = val.astype(BF)
            send(
                SB.at[k, way, s], YB.at[k, way, s], rs, (k, way, s),
                dev(dy=1 if way == 0 else -1),
            )

    own_sum(7)
    for k in range(C):
        reduce(k, k % 2, 0)
    own_sum(6)
    for k in range(C):
        if k % 2 == 1:
            reduce(k, 0, 0)
    own_sum(5)
    for k in range(C):
        if k % 2 == 0:
            reduce(k, 1, 0)
    for s in range(1, 4):
        for n in ((4, 3), (2, 1), (0,))[s - 1]:
            own_sum(n)
        for k in range(C):
            for way in (k % 2, 1 - k % 2):
                reduce(k, way, s)
    for k in range(C):
        cols = slice(W * k, W * (k + 1))
        total = HB[:, cols] + PS[y, k]
        for way in (1 - k % 2, k % 2):
            total = total + take(k, way, far[k][way])
        out_ref[:, cols] = total.astype(BF)
    for cp in sent:
        cp.wait_send()


def hand_on(att_in, out_in, att_ref, out_ref):
    att_ref[...] = att_in[...]
    out_ref[...] = out_in[...]


def per_device(
    x_resid, q_latent, q_rope, cache_latent, cache_rope, new_latent, new_rope, w_uv, w_out,
    norm_gain, router, expert_ids, w_gate, w_up, w_down,
):
    vmem = pl.BlockSpec(memory_space=pltpu.VMEM)
    anyspace = pl.BlockSpec(memory_space=pl.ANY)
    dma = pltpu.SemaphoreType.DMA
    att, out = pl.pallas_call(
        kernel,
        out_shape=(jax.ShapeDtypeStruct((64, 2048), BF), jax.ShapeDtypeStruct((64, 2048), BF)),
        in_specs=[vmem] * 12 + [anyspace] * 3,
        out_specs=(vmem, vmem),
        scratch_shapes=[
            pltpu.VMEM((8, 16, 2, 80, 128), BF),
            pltpu.VMEM((704, 2048), BF),
            pltpu.VMEM((704, 2048), BF),
            pltpu.VMEM((704, 2048), BF),
            pltpu.VMEM((128, 512), BF),
            pltpu.VMEM((128, 64), BF),
            pltpu.VMEM((512, 128), BF),
            pltpu.VMEM((512, 512), BF),
            pltpu.VMEM((64, 1024), BF),
            pltpu.VMEM((64, 2048), F32),
            pltpu.VMEM((RY, C, 64, W), BF),
            pltpu.VMEM((RY, 64, 128), BF),
            pltpu.VMEM((RY, 4, 64, 128), BF),
            pltpu.VMEM((RY, 64, W), BF),
            pltpu.VMEM((RY, 3, PAD, 1536), BF),
            pltpu.VMEM((RY, 4, PAD, 1536), BF),
            pltpu.VMEM((RY, 4, PAD, 1536), BF),
            pltpu.VMEM((RY, 4, PAD, 1536), BF),
            pltpu.VMEM((RY, C, 64, W), F32),
            pltpu.VMEM((C, 2, 4, 64, W), BF),
            pltpu.VMEM((C, 2, 4, 64, W), BF),
            dma((3,)),
            dma((2, 6)),
            dma((2, 1)),
            dma((2, 2, RY)),
            dma((2, 2, 2, 4)),
            dma((2, RY, 4)),
            dma((2, C, 2, 4)),
            dma((2, 2, 4)),
            dma((2, RY, 3)),
            dma((2, RY, 3)),
            dma((2, C, 2, 4)),
        ],
        compiler_params=pltpu.CompilerParams(
            collective_id=0, has_side_effects=True, vmem_limit_bytes=56 << 20
        ),
    )(
        x_resid[0],
        q_latent.reshape(512, 512),
        q_rope.reshape(512, 64),
        cache_latent[0],
        cache_rope[0],
        new_latent[0],
        new_rope[0],
        w_uv,
        w_out,
        norm_gain.reshape(1, 2048),
        router.T,
        jnp.transpose(expert_ids, (2, 0, 1)),
        w_gate[0].T,
        w_up[0].T,
        w_down[0],
    )
    att, out = pl.pallas_call(
        hand_on,
        out_shape=(jax.ShapeDtypeStruct((64, 2048), BF), jax.ShapeDtypeStruct((64, 2048), BF)),
        in_specs=[vmem] * 2,
        out_specs=(vmem, vmem),
    )(att, out)
    return att[None], out[None]


def solution(mesh):
    seq = P(("fsdp", "ep"), None, None)
    placed = (
        seq,
        P(("fsdp", "ep"), None, None, None),
        P(("fsdp", "ep"), None, None, None),
        seq,
        seq,
        seq,
        seq,
        P("fsdp", None, None),
        P("fsdp", None),
        P(),
        P(),
        seq,
        P("ep", None, None),
        P("ep", None, None),
        P("ep", None, None),
    )
    return jax.shard_map(
        per_device, mesh=mesh, in_specs=placed, out_specs=(seq, seq), check_vma=False
    )
```
